1024 devices in a mesh: dp: 4 (over x_hi, core), shard: 256 (over y, z, x_lo).
Axes of the slice: x: 4 (x_hi: 2, x_lo: 2; x = x_hi * 2 + x_lo), y: 4, z: 32, core: 2. Of those that a mesh axis runs over, the one named last changes fastest.
Arguments:
- activations: bfloat16 [131072, 4096], P(('dp', 'shard')), may hold values from -24 to 24
- w_query: bfloat16 [4096, 128], P('shard'), may hold values from -0.09375 to 0.09375
- w_key: bfloat16 [4096, 128], P('shard'), may hold values from -0.09375 to 0.09375
- grad_query: bfloat16 [131072, 128], P(('dp', 'shard')), may hold values from -12 to 12
- grad_key: bfloat16 [131072, 128], P(('dp', 'shard')), may hold values from -12 to 12
Outputs:
- query_out: bfloat16 [131072, 128], P(('dp', 'shard'))
- key_out: bfloat16 [131072, 128], P(('dp', 'shard'))
- grad_input: bfloat16 [131072, 4096], P(('dp', 'shard'))
- grad_w_query: float32 [4096, 128], P('shard')
- grad_w_key: float32 [4096, 128], P('shard')
The draws below stay inside these ranges and needn't reach their ends.
All inputs are finite; a program needn't handle non-finite values.
Results may differ from the reference program's by a relative error of at most 0.001.
Values may be sent and summed in bfloat16 or wider, within the bound.
No kernel may reach another device: no remote copies, remote signals or barrier semaphores. Data moves between devices by JAX's collectives and lax.ppermute only.
A program may use at most 64 MiB of HBM per device.

```python
import math
import jax
import jax.numpy as jnp
from jax import lax

D = 4096
HEAD = 128
TOK_DEV = 128
TOKENS = 131072


def with_spikes(entries, stream_key, source, target, shards_of, factor):
    def block_of(position):
        return (jnp.arange(entries.shape[position]) // (entries.shape[position] // shards_of)).reshape((-1,) + (1,) * (entries.ndim - 1 - position))

    near = jax.random.permutation(stream_key, shards_of)[block_of(target)]
    second = (block_of(target) + shards_of // 2) % shards_of
    return jnp.where((block_of(source) == near) | (block_of(source) == second), factor * entries, entries)


def level_of(own_key, shape, pieces, smallest, high):
    level = 1.0
    for position, parts in pieces:
        heights = jax.random.uniform(jax.random.fold_in(jax.random.fold_in(own_key, 6), position), (parts,), jnp.float32, smallest / len(pieces), high / len(pieces))
        level = level * jnp.repeat(jnp.exp(heights), shape[position] // parts).reshape((-1,) + (1,) * (len(shape) - 1 - position))
    return level


def centred(own_key, dims, scale, reach, cuts=(), kind=jnp.bfloat16):
    gain = level_of(own_key, dims, cuts, -0.22, 0.18) if cuts else 1.0
    values = jax.random.normal(own_key, dims, jnp.float32) * scale * gain
    return jnp.minimum(jnp.maximum(values, -reach), reach).astype(kind)


def heavy_noise(key, dims, scale, limit, split, heavy, kind=jnp.bfloat16):
    values = scale * jax.random.normal(key, dims, jnp.float32)
    if split:
        values = values * level_of(key, dims, split, -0.22, 0.18)
    return jnp.clip(with_spikes(values, jax.random.fold_in(key, 3), *heavy), -limit, limit).astype(kind)


def setup_inputs(seed: int = 0) -> dict:
    seeds = jax.random.split(jax.random.key(seed), 6)
    return {
        "activations": heavy_noise(seeds[0], (TOKENS, D), 1.0, 24.0, ((0, 1024),), (0, 1, 1024, 6.0)),
        "w_query": centred(seeds[1], (D, HEAD), D ** -0.5, 0.09375, ((0, 256),)),
        "w_key": centred(seeds[2], (D, HEAD), D ** -0.5, 0.09375, ((0, 256),)),
        "grad_query": centred(seeds[3], (TOKENS, HEAD), 2.0, 12.0, ((0, 1024),)),
        "grad_key": centred(seeds[4], (TOKENS, HEAD), 2.0, 12.0, ((0, 1024),)),
    }


def reference(activations, w_query, w_key, grad_query, grad_key):
    head_size = w_query.shape[1]
    width = activations.shape[1]
    weights = jnp.concatenate([w_query, w_key], axis=1)
    cotangent = jnp.concatenate([grad_query, grad_key], axis=1)
    blocks = activations.shape[0] // TOK_DEV
    act_blocks = activations.reshape(blocks, TOK_DEV, width)
    cot_blocks = cotangent.reshape(blocks, TOK_DEV, 2 * head_size)

    def step(summed, pair):
        act_block, cot_block = pair
        projected = jnp.dot(act_block, weights, preferred_element_type=jnp.float32).astype(jnp.bfloat16)
        backward = lax.dot_general(cot_block, weights, (((1,), (1,)), ((), ())), preferred_element_type=jnp.float32).astype(jnp.bfloat16)
        partial_sum = lax.dot_general(act_block, cot_block, (((0,), (0,)), ((), ())), preferred_element_type=jnp.float32)
        return (summed + partial_sum, (projected, backward))
    start_sum = jnp.zeros((width, 2 * head_size), jnp.float32)
    summed, outputs = lax.scan(step, start_sum, (act_blocks, cot_blocks))
    projected, backward = outputs
    projected = projected.reshape(activations.shape[0], 2 * head_size)
    grad_input = backward.reshape(activations.shape[0], width)
    factor = 1.0 / math.sqrt(activations.shape[0])
    summed = summed * factor
    return (projected[:, :head_size], projected[:, head_size:], grad_input, summed[:, :head_size], summed[:, head_size:])
```

```python
import math

import jax
import jax.numpy as jnp
from jax import lax
from jax.sharding import Mesh, PartitionSpec as P

PLANE = ("xh", "y", "xl")


def swap_cores(block):
    return lax.ppermute(block, "c", [(0, 1), (1, 0)])


def pick(first, second):
    return lax.select(lax.axis_index("c") == 0, first, second)


def spread(block, axes, count):
    copies = jnp.broadcast_to(block[None], (count,) + block.shape)
    return lax.all_to_all(copies, axes, 0, 0, tiled=True)


def body(activations, w_query, w_key, grad_query, grad_key):
    width = activations.shape[1]
    head = w_query.shape[1]
    xh, cores, ys, zs, xl = (lax.axis_size(a) for a in ("xh", "c", "y", "z", "xl"))
    rows = w_query.shape[0]
    half = rows // xh
    plane = xh * ys * xl
    tokens = activations.shape[0] * plane * cores * zs
    factor = 1.0 / math.sqrt(tokens)

    def terms(cotangent):
        return lax.dot_general(
            activations, cotangent, (((0,), (0,)), ((), ())), preferred_element_type=jnp.float32
        )

    mine = pick(grad_query, grad_key)
    other = pick(grad_key, grad_query)
    arrived = swap_cores(terms(other))
    own = pick(w_query, w_key)
    own = lax.dynamic_slice_in_dim(own, lax.axis_index("xh") * half, half, 0)
    column = spread(own, "z", zs)
    sheet = spread(column, PLANE, plane)
    sheet = sheet.reshape(xh, ys, xl, zs, half, head).transpose(1, 3, 2, 0, 4, 5).reshape(width, head)
    other_sheet = swap_cores(sheet)
    wq = pick(sheet, other_sheet)
    wk = pick(other_sheet, sheet)

    paired = terms(mine) + arrived
    paired = paired.reshape(ys, zs, xl, xh, half, head).transpose(3, 0, 2, 1, 4, 5)
    paired = paired.reshape(plane, zs, half, head)
    summed = lax.all_to_all(paired, PLANE, 0, 0, tiled=True).sum(axis=0)
    summed = lax.all_to_all(summed, "z", 0, 0, tiled=True).sum(axis=0) * factor
    whole = lax.all_gather(summed, ("c", "xh"), axis=0, tiled=True)

    weights = jnp.concatenate([wq, wk], axis=1)
    cotangent = jnp.concatenate([grad_query, grad_key], axis=1)
    projected = jnp.dot(activations, weights, preferred_element_type=jnp.float32).astype(jnp.bfloat16)
    grad_input = lax.dot_general(
        cotangent, weights, (((1,), (1,)), ((), ())), preferred_element_type=jnp.float32
    ).astype(jnp.bfloat16)
    return (projected[:, :head], projected[:, head:], grad_input, whole[:rows], whole[rows:])


def solution(mesh):
    shape = (2, 2, 4, mesh.shape["shard"] // 8, 2)
    fine = Mesh(mesh.devices.reshape(shape), ("xh", "c", "y", "z", "xl"))
    tokens = P(("xh", "c", "y", "z", "xl"), None)
    weights = P(("y", "z", "xl"), None)
    return jax.shard_map(
        body,
        mesh=fine,
        in_specs=(tokens, weights, weights, tokens, tokens),
        out_specs=(tokens, tokens, tokens, weights, weights),
        check_vma=False,
    )
```

```python
import math

import jax
import jax.numpy as jnp
from jax import lax
from jax.experimental import pallas as pl
from jax.experimental.pallas import tpu as pltpu
from jax.sharding import Mesh, PartitionSpec as P

PLANE = ("xh", "y", "xl")


def swap_cores(block):
    return lax.ppermute(block, "c", [(0, 1), (1, 0)])


def pick(first, second):
    return lax.select(lax.axis_index("c") == 0, first, second)


def terms_kernel(act_ref, cot_ref, *refs):
    out_ref = refs[-1]
    xh, _, xl, zs, half, head = out_ref.shape
    part = lax.dot_general(
        act_ref[...], cot_ref[...], (((0,), (0,)), ((), ())), preferred_element_type=jnp.float32
    ).reshape(zs, xl, xh, half, head)
    for i in range(xh):
        for j in range(xl):
            piece = part[:, j, i]
            if len(refs) == 2:
                piece = piece + refs[0][i, 0, j]
            out_ref[i, 0, j] = piece


def terms(activations, cotangent, arrived=None):
    tokens, width = activations.shape
    head = cotangent.shape[1]
    ys, zs = lax.axis_size("y"), lax.axis_size("z")
    cut = 2
    block = width // (ys * cut)
    half = width // (4 * ys * zs)
    spread = pl.BlockSpec((2, 1, 2, zs // cut, half, head), lambda y, z: (0, y, 0, z, 0, 0))
    operands = [activations, cotangent] + ([] if arrived is None else [arrived])
    return pl.pallas_call(
        terms_kernel,
        grid=(ys, cut),
        in_specs=[
            pl.BlockSpec((tokens, block), lambda y, z: (0, y * cut + z)),
            pl.BlockSpec((tokens, head), lambda y, z: (0, 0)),
        ]
        + [spread] * (len(operands) - 2),
        out_specs=spread,
        out_shape=jax.ShapeDtypeStruct((2, ys, 2, zs, half, head), jnp.float32),
        cost_estimate=pl.CostEstimate(
            flops=2 * tokens * width * head, bytes_accessed=6 * width * head, transcendentals=0
        ),
    )(*operands)


def body(activations, w_query, w_key, grad_query, grad_key):
    width = activations.shape[1]
    rows, head = w_query.shape
    ys, zs = lax.axis_size("y"), lax.axis_size("z")
    half = rows // 2
    plane = 4 * ys
    factor = 1.0 / math.sqrt(activations.shape[0] * 2 * plane * zs)

    mine = pick(grad_query, grad_key)
    other = pick(grad_key, grad_query)
    arrived = swap_cores(terms(activations, other))
    paired = terms(activations, mine, arrived).reshape(plane, zs, half, head)
    summed = lax.all_to_all(paired, PLANE, 0, 0, tiled=True).sum(axis=0)

    own = pick(w_query, w_key)
    own = lax.dynamic_slice_in_dim(own, lax.axis_index("xh") * half, half, 0)
    high = lax.reduce_precision(summed, 8, 7)
    low = summed - high
    sent = jnp.concatenate(
        [jnp.broadcast_to(own[None], (zs, half, head)), high.astype(jnp.bfloat16), low.astype(jnp.bfloat16)],
        axis=1,
    )
    landed = lax.all_to_all(sent, "z", 0, 0, tiled=True)
    column = landed[:, :half]
    summed = landed[:, half:].astype(jnp.float32)
    summed = (summed[:, :half] + summed[:, half:]).sum(axis=0) * factor

    sheet = lax.all_to_all(
        jnp.broadcast_to(column[None], (plane, zs, half, head)), PLANE, 0, 0, tiled=True
    )
    whole = lax.all_gather(summed, ("c", "xh"), axis=0, tiled=True)
    sheet = sheet.reshape(2, ys, 2, zs, half, head).transpose(1, 3, 2, 0, 4, 5).reshape(width, head)
    other_sheet = swap_cores(sheet)

    weights = jnp.concatenate([sheet, other_sheet], axis=1)
    cotangent = jnp.concatenate([mine, other], axis=1)
    projected = jnp.dot(activations, weights, preferred_element_type=jnp.float32).astype(jnp.bfloat16)
    grad_input = lax.dot_general(
        cotangent, weights, (((1,), (1,)), ((), ())), preferred_element_type=jnp.float32
    ).astype(jnp.bfloat16)
    first, second = projected[:, :head], projected[:, head:]
    return (pick(first, second), pick(second, first), grad_input, whole[:rows], whole[rows:])


def solution(mesh):
    names = ("xh", "c", "y", "z", "xl")
    shape = (2, 2, 4, mesh.shape["shard"] // 8, 2)
    fine = Mesh(mesh.devices.reshape(shape), names)
    tokens = P(names, None)
    weights = P(("y", "z", "xl"), None)
    return jax.shard_map(
        body,
        mesh=fine,
        in_specs=(tokens, weights, weights, tokens, tokens),
        out_specs=(tokens, tokens, tokens, weights, weights),
        check_vma=False,
    )
```

```python
import math

import jax
import jax.numpy as jnp
from jax import lax
from jax.experimental import pallas as pl
from jax.experimental.pallas import tpu as pltpu
from jax.sharding import Mesh, PartitionSpec as P

PLANE = ("xh", "y", "xl")
NEAR = ("xh", "y", "zl", "xl")


def swap_cores(block):
    return lax.ppermute(block, "c", [(0, 1), (1, 0)])


def pick(first, second):
    return lax.select(lax.axis_index("c") == 0, first, second)


def exchange(blocks, axes):
    return lax.all_to_all(blocks, axes, 0, 0, tiled=True)


def copies(block, count):
    return jnp.broadcast_to(block[None], (count,) + block.shape)


def terms_kernel(lows, act_ref, cot_ref, *refs):
    out_ref = refs[-1]
    _, ys, _, tiles, half, head = out_ref.shape
    zs = tiles - tiles % 2
    highs = zs // lows
    cut = 2
    span = highs // cut
    block = act_ref.shape[1] // (ys * cut)
    peak = jnp.zeros((half, head), jnp.float32)
    for y in range(ys):
        for z in range(cut):
            start = (y * cut + z) * block
            part = lax.dot_general(
                act_ref[:, start : start + block],
                cot_ref[...],
                (((0,), (0,)), ((), ())),
                preferred_element_type=jnp.float32,
            ).reshape(span, lows, 2, 2, half, head)
            for i in range(2):
                for j in range(2):
                    for low in range(lows):
                        place = low * highs + z * span
                        piece = part[:, low, j, i]
                        if len(refs) == 2:
                            piece = piece + refs[0][i, y, j, place : place + span]
                            peak = jnp.maximum(peak, jnp.abs(piece).max(axis=0))
                        out_ref[i, y, j, place : place + span] = piece
    if len(refs) == 2:
        top = jnp.broadcast_to(jnp.max(peak, keepdims=True), (half, head))
        level = jnp.floor(jnp.log2(32768.0 / jnp.maximum(top, 1e-30)))
        scale = jnp.exp2(level)
        for i in range(2):
            for y in range(ys):
                for j in range(2):
                    out_ref[i, y, j, :zs] = out_ref[i, y, j, :zs] * scale[None]
                    out_ref[i, y, j, zs] = level


def terms(activations, cotangent, *arrived):
    tokens, width = activations.shape
    head = cotangent.shape[1]
    ys, lows = lax.axis_size("y"), lax.axis_size("zl")
    zs = lows * lax.axis_size("zh")
    half = width // (4 * ys * zs)
    return pl.pallas_call(
        lambda *refs: terms_kernel(lows, *refs),
        out_shape=jax.ShapeDtypeStruct((2, ys, 2, zs + len(arrived), half, head), jnp.float32),
        compiler_params=pltpu.CompilerParams(vmem_limit_bytes=40 * 2**20),
        cost_estimate=pl.CostEstimate(
            flops=2 * tokens * width * head, bytes_accessed=6 * width * head, transcendentals=0
        ),
    )(activations, cotangent, *arrived)


def body(activations, w_query, w_key, grad_query, grad_key):
    width = activations.shape[1]
    rows, head = w_query.shape
    ys, highs, lows = (lax.axis_size(a) for a in ("y", "zh", "zl"))
    half = rows // 2
    plane = 4 * ys
    factor = 1.0 / math.sqrt(activations.shape[0] * 2 * plane * highs * lows)

    mine = pick(grad_query, grad_key)
    other = pick(grad_key, grad_query)
    arrived = swap_cores(terms(activations, other))
    sent = terms(activations, mine, arrived).astype(jnp.float16)
    landed = exchange(sent.reshape((plane,) + sent.shape[3:]), PLANE).astype(jnp.float32)
    summed = (landed[:, :-1] * jnp.exp2(-landed[:, -1:])).sum(axis=0)
    summed = exchange(summed.reshape(lows, highs, half, head), "zl").sum(axis=0)

    own = pick(w_query, w_key)
    own = lax.dynamic_slice_in_dim(own, lax.axis_index("xh") * half, half, 0)
    high = lax.reduce_precision(summed, 8, 7)
    parts = [copies(own, highs), high.astype(jnp.bfloat16), (summed - high).astype(jnp.bfloat16)]
    landed = exchange(jnp.concatenate(parts, axis=1), "zh")
    column = landed[:, :half]
    summed = landed[:, half:].astype(jnp.float32)
    summed = (summed[:, :half] + summed[:, half:]).sum(axis=0) * factor

    sheet = exchange(copies(column, plane * lows), NEAR)
    whole = lax.all_gather(summed, ("c", "xh"), axis=0, tiled=True)
    sheet, whole = lax.optimization_barrier((sheet, whole))
    sheet = sheet.reshape(2, ys, lows, 2, highs, half, head).transpose(1, 4, 2, 3, 0, 5, 6)
    sheet = sheet.reshape(width, head)
    other_sheet = swap_cores(sheet)

    weights = jnp.concatenate([sheet, other_sheet], axis=1)
    cotangent = jnp.concatenate([mine, other], axis=1)
    projected = jnp.dot(activations, weights, preferred_element_type=jnp.float32).astype(jnp.bfloat16)
    grad_input = lax.dot_general(
        cotangent, weights, (((1,), (1,)), ((), ())), preferred_element_type=jnp.float32
    ).astype(jnp.bfloat16)
    first, second = projected[:, :head], projected[:, head:]
    return (pick(first, second), pick(second, first), grad_input, whole[:rows], whole[rows:])


def solution(mesh):
    names = ("xh", "c", "y", "zh", "zl", "xl")
    shape = (2, 2, 4, mesh.shape["shard"] // 32, 4, 2)
    fine = Mesh(mesh.devices.reshape(shape), names)
    tokens = P(names, None)
    weights = P(("y", "zh", "zl", "xl"), None)
    return jax.shard_map(
        body,
        mesh=fine,
        in_specs=(tokens, weights, weights, tokens, tokens),
        out_specs=(tokens, tokens, tokens, weights, weights),
        check_vma=False,
    )
```

```python
import math

import jax
import jax.numpy as jnp
from jax import lax
from jax.experimental import pallas as pl
from jax.experimental.pallas import tpu as pltpu
from jax.sharding import Mesh, PartitionSpec as P

NEAR = ("xh", "y", "xl", "zl")


def swap_cores(block):
    return lax.ppermute(block, "c", [(0, 1), (1, 0)])


def pick(first, second):
    return lax.select(lax.axis_index("c") == 0, first, second)


def exchange(blocks, axes):
    return lax.all_to_all(blocks, axes, 0, 0, tiled=True)


def copies(block, count):
    return jnp.broadcast_to(block[None], (count,) + block.shape)


def terms_kernel(highs, act_ref, cot_ref, *refs):
    out_ref = refs[-1]
    _, ys, _, lows, _, half, head = out_ref.shape
    cut = 2
    span = highs // cut
    block = act_ref.shape[1] // (ys * cut)
    peak = jnp.zeros((half, head), jnp.float32)
    for y in range(ys):
        for z in range(cut):
            start = (y * cut + z) * block
            part = lax.dot_general(
                act_ref[:, start : start + block],
                cot_ref[...],
                (((0,), (0,)), ((), ())),
                preferred_element_type=jnp.float32,
            ).reshape(span, lows, 2, 2, half, head)
            for i in range(2):
                for j in range(2):
                    for low in range(lows):
                        piece = part[:, low, j, i]
                        if len(refs) == 2:
                            piece = piece + refs[0][i, y, j, low, z * span : (z + 1) * span]
                            peak = jnp.maximum(peak, jnp.abs(piece).max(axis=0))
                        out_ref[i, y, j, low, z * span : (z + 1) * span] = piece
    if len(refs) == 2:
        top = jnp.broadcast_to(jnp.max(peak, keepdims=True), (half, head))
        level = jnp.floor(jnp.log2(32768.0 / jnp.maximum(top, 1e-30)))
        scale = jnp.exp2(level)
        for i in range(2):
            for y in range(ys):
                for j in range(2):
                    for low in range(lows):
                        out_ref[i, y, j, low, :highs] = out_ref[i, y, j, low, :highs] * scale[None]
                        out_ref[i, y, j, low, highs] = level


def terms(activations, cotangent, *arrived):
    tokens, width = activations.shape
    head = cotangent.shape[1]
    ys, lows, highs = (lax.axis_size(a) for a in ("y", "zl", "zh"))
    half = width // (4 * ys * lows * highs)
    return pl.pallas_call(
        lambda *refs: terms_kernel(highs, *refs),
        out_shape=jax.ShapeDtypeStruct(
            (2, ys, 2, lows, highs + len(arrived), half, head), jnp.float32
        ),
        compiler_params=pltpu.CompilerParams(vmem_limit_bytes=40 * 2**20),
        cost_estimate=pl.CostEstimate(
            flops=2 * tokens * width * head, bytes_accessed=6 * width * head, transcendentals=0
        ),
    )(activations, cotangent, *arrived)


def body(activations, w_query, w_key, grad_query, grad_key):
    width = activations.shape[1]
    rows, head = w_query.shape
    ys, highs, lows = (lax.axis_size(a) for a in ("y", "zh", "zl"))
    half = rows // 2
    near = 4 * ys * lows
    factor = 1.0 / math.sqrt(activations.shape[0] * 2 * near * highs)

    mine = pick(grad_query, grad_key)
    other = pick(grad_key, grad_query)
    arrived = swap_cores(terms(activations, other))
    sent = terms(activations, mine, arrived).astype(jnp.float16)
    landed = exchange(sent.reshape((near,) + sent.shape[4:]), NEAR).astype(jnp.float32)
    summed = (landed[:, :-1] * jnp.exp2(-landed[:, -1:])).sum(axis=0)

    own = pick(w_query, w_key)
    own = lax.dynamic_slice_in_dim(own, lax.axis_index("xh") * half, half, 0)
    high = lax.reduce_precision(summed, 8, 7)
    parts = [copies(own, highs), high.astype(jnp.bfloat16), (summed - high).astype(jnp.bfloat16)]
    landed = exchange(jnp.concatenate(parts, axis=1), "zh")
    column = landed[:, :half]
    summed = landed[:, half:].astype(jnp.float32)
    summed = (summed[:, :half] + summed[:, half:]).sum(axis=0) * factor

    sheet = exchange(copies(column, near), NEAR)
    whole = lax.all_gather(summed, ("c", "xh"), axis=0, tiled=True)
    sheet, whole = lax.optimization_barrier((sheet, whole))
    sheet = sheet.reshape(2, ys, 2, lows, highs, half, head).transpose(1, 4, 3, 2, 0, 5, 6)
    sheet = sheet.reshape(width, head)
    other_sheet = swap_cores(sheet)

    weights = jnp.concatenate([sheet, other_sheet], axis=1)
    cotangent = jnp.concatenate([mine, other], axis=1)
    projected = jnp.dot(activations, weights, preferred_element_type=jnp.float32).astype(jnp.bfloat16)
    grad_input = lax.dot_general(
        cotangent, weights, (((1,), (1,)), ((), ())), preferred_element_type=jnp.float32
    ).astype(jnp.bfloat16)
    first, second = projected[:, :head], projected[:, head:]
    return (pick(first, second), pick(second, first), grad_input, whole[:rows], whole[rows:])


def solution(mesh):
    names = ("xh", "c", "y", "zh", "zl", "xl")
    shape = (2, 2, 4, mesh.shape["shard"] // 16, 2, 2)
    fine = Mesh(mesh.devices.reshape(shape), names)
    tokens = P(names, None)
    weights = P(("y", "zh", "zl", "xl"), None)
    return jax.shard_map(
        body,
        mesh=fine,
        in_specs=(tokens, weights, weights, tokens, tokens),
        out_specs=(tokens, tokens, tokens, weights, weights),
        check_vma=False,
    )
```

```python
import math

import jax
import jax.numpy as jnp
from jax import lax
from jax.experimental import pallas as pl
from jax.experimental.pallas import tpu as pltpu
from jax.sharding import Mesh, PartitionSpec as P

NEAR = ("xh", "y", "xl", "zl")


def swap(block, axis):
    return lax.ppermute(block, axis, [(0, 1), (1, 0)])


def ordered(own, came, axis):
    first = lax.axis_index(axis) == 0
    return lax.select(first, own, came), lax.select(first, came, own)


def pick(first, second):
    return lax.select(lax.axis_index("c") == 0, first, second)


def exchange(blocks, axes):
    return lax.all_to_all(blocks, axes, 0, 0, tiled=True)


def copies(block, count):
    return jnp.broadcast_to(block[None], (count,) + block.shape)


def terms_kernel(highs, act_ref, cot_ref, *refs):
    out_ref = refs[-1]
    _, ys, _, lows, _, half, head = out_ref.shape
    cut = 2
    span = highs // cut
    block = act_ref.shape[1] // (ys * cut)
    peak = jnp.zeros((half, head), jnp.float32)
    for y in range(ys):
        for z in range(cut):
            start = (y * cut + z) * block
            part = lax.dot_general(
                act_ref[:, start : start + block],
                cot_ref[...],
                (((0,), (0,)), ((), ())),
                preferred_element_type=jnp.float32,
            ).reshape(span, lows, 2, 2, half, head)
            for i in range(2):
                for j in range(2):
                    for low in range(lows):
                        piece = part[:, low, j, i]
                        if len(refs) == 2:
                            piece = piece + refs[0][i, y, j, low, z * span : (z + 1) * span]
                            peak = jnp.maximum(peak, jnp.abs(piece).max(axis=0))
                        out_ref[i, y, j, low, z * span : (z + 1) * span] = piece
    if len(refs) == 2:
        top = jnp.broadcast_to(jnp.max(peak, keepdims=True), (half, head))
        level = jnp.floor(jnp.log2(32768.0 / jnp.maximum(top, 1e-30)))
        scale = jnp.exp2(level)
        for i in range(2):
            for y in range(ys):
                for j in range(2):
                    for low in range(lows):
                        out_ref[i, y, j, low, :highs] = out_ref[i, y, j, low, :highs] * scale[None]
                        out_ref[i, y, j, low, highs] = level


def terms(activations, cotangent, *arrived):
    tokens, width = activations.shape
    head = cotangent.shape[1]
    ys, lows, highs = (lax.axis_size(a) for a in ("y", "zl", "zh"))
    half = width // (4 * ys * lows * highs)
    return pl.pallas_call(
        lambda *refs: terms_kernel(highs, *refs),
        out_shape=jax.ShapeDtypeStruct(
            (2, ys, 2, lows, highs + len(arrived), half, head), jnp.float32
        ),
        compiler_params=pltpu.CompilerParams(vmem_limit_bytes=40 * 2**20),
        cost_estimate=pl.CostEstimate(
            flops=2 * tokens * width * head, bytes_accessed=6 * width * head, transcendentals=0
        ),
    )(activations, cotangent, *arrived)


def body(activations, w_query, w_key, grad_query, grad_key):
    width = activations.shape[1]
    rows, head = w_query.shape
    ys, highs, lows = (lax.axis_size(a) for a in ("y", "zh", "zl"))
    half = rows // 2
    near = 4 * ys * lows
    factor = 1.0 / math.sqrt(activations.shape[0] * 2 * near * highs)

    mine = pick(grad_query, grad_key)
    other = pick(grad_key, grad_query)
    arrived = swap(terms(activations, other), "c")
    sent = terms(activations, mine, arrived).astype(jnp.float16)
    landed = exchange(sent.reshape((near,) + sent.shape[4:]), NEAR).astype(jnp.float32)
    summed = (landed[:, :-1] * jnp.exp2(-landed[:, -1:])).sum(axis=0)

    own = pick(w_query, w_key)
    own = lax.dynamic_slice_in_dim(own, lax.axis_index("xh") * half, half, 0)
    high = lax.reduce_precision(summed, 8, 7)
    parts = [copies(own, highs), high.astype(jnp.bfloat16), (summed - high).astype(jnp.bfloat16)]
    landed = exchange(jnp.concatenate(parts, axis=1), "zh")
    column = landed[:, :half]
    summed = landed[:, half:].astype(jnp.float32)
    summed = (summed[:, :half] + summed[:, half:]).sum(axis=0) * factor

    sheet = exchange(copies(column, near), NEAR)
    both = jnp.stack(ordered(summed, swap(summed, "c"), "c"))
    whole = jnp.concatenate(ordered(both, swap(both, "xh"), "xh"), axis=1)
    sheet, whole = lax.optimization_barrier((sheet, whole))
    sheet = sheet.reshape(2, ys, 2, lows, highs, half, head).transpose(1, 4, 3, 2, 0, 5, 6)
    sheet = sheet.reshape(width, head)
    other_sheet = swap(sheet, "c")

    weights = jnp.concatenate([sheet, other_sheet], axis=1)
    cotangent = jnp.concatenate([mine, other], axis=1)
    projected = jnp.dot(activations, weights, preferred_element_type=jnp.float32).astype(jnp.bfloat16)
    grad_input = lax.dot_general(
        cotangent, weights, (((1,), (1,)), ((), ())), preferred_element_type=jnp.float32
    ).astype(jnp.bfloat16)
    first, second = projected[:, :head], projected[:, head:]
    return (pick(first, second), pick(second, first), grad_input, whole[0], whole[1])


def solution(mesh):
    names = ("xh", "c", "y", "zh", "zl", "xl")
    shape = (2, 2, 4, mesh.shape["shard"] // 16, 2, 2)
    fine = Mesh(mesh.devices.reshape(shape), names)
    tokens = P(names, None)
    weights = P(("y", "zh", "zl", "xl"), None)
    return jax.shard_map(
        body,
        mesh=fine,
        in_specs=(tokens, weights, weights, tokens, tokens),
        out_specs=(tokens, tokens, tokens, weights, weights),
        check_vma=False,
    )
```

```python
import math

import jax
import jax.numpy as jnp
from jax import lax
from jax.experimental import pallas as pl
from jax.experimental.pallas import tpu as pltpu
from jax.sharding import Mesh, PartitionSpec as P

NEAR = ("xh", "y", "xl", "zl")


def swap(block, axis):
    return lax.ppermute(block, axis, [(0, 1), (1, 0)])


def ordered(own, came, axis):
    first = lax.axis_index(axis) == 0
    return lax.select(first, own, came), lax.select(first, came, own)


def pick(first, second):
    return lax.select(lax.axis_index("c") == 0, first, second)


def exchange(blocks, axes):
    return lax.all_to_all(blocks, axes, 0, 0, tiled=True)


def copies(block, count):
    return jnp.broadcast_to(block[None], (count,) + block.shape)


def terms_kernel(highs, act_ref, cot_ref, *refs):
    out_ref = refs[-1]
    _, ys, _, lows, _, half, head = out_ref.shape
    cut = 2
    span = highs // cut
    block = act_ref.shape[1] // (ys * cut)
    peak = jnp.zeros((half, head), jnp.float32)
    for y in range(ys):
        for z in range(cut):
            start = (y * cut + z) * block
            part = lax.dot_general(
                act_ref[:, start : start + block],
                cot_ref[...],
                (((0,), (0,)), ((), ())),
                preferred_element_type=jnp.float32,
            ).reshape(span, lows, 2, 2, half, head)
            for i in range(2):
                for j in range(2):
                    for low in range(lows):
                        piece = part[:, low, j, i]
                        if len(refs) == 2:
                            piece = piece + refs[0][i, y, j, low, z * span : (z + 1) * span]
                            peak = jnp.maximum(peak, jnp.abs(piece).max(axis=0))
                        out_ref[i, y, j, low, z * span : (z + 1) * span] = piece
    if len(refs) == 2:
        top = jnp.broadcast_to(jnp.max(peak, keepdims=True), (half, head))
        level = jnp.floor(jnp.log2(32768.0 / jnp.maximum(top, 1e-30)))
        scale = jnp.exp2(level)
        for i in range(2):
            for y in range(ys):
                for j in range(2):
                    for low in range(lows):
                        out_ref[i, y, j, low, :highs] = out_ref[i, y, j, low, :highs] * scale[None]
                        out_ref[i, y, j, low, highs] = level


def terms(activations, cotangent, *others):
    tokens, width = activations.shape
    head = cotangent.shape[1]
    ys, lows, highs = (lax.axis_size(a) for a in ("y", "zl", "zh"))
    half = width // (4 * ys * lows * highs)
    return pl.pallas_call(
        lambda *refs: terms_kernel(highs, *refs),
        out_shape=jax.ShapeDtypeStruct(
            (2, ys, 2, lows, highs + len(others), half, head), jnp.float32
        ),
        compiler_params=pltpu.CompilerParams(vmem_limit_bytes=40 * 2**20),
        cost_estimate=pl.CostEstimate(
            flops=2 * tokens * width * head, bytes_accessed=6 * width * head, transcendentals=0
        ),
    )(activations, cotangent, *others)


def body(activations, w_query, w_key, grad_query, grad_key):
    width = activations.shape[1]
    rows, head = w_query.shape
    ys, highs, lows = (lax.axis_size(a) for a in ("y", "zh", "zl"))
    half = rows // 2
    near = 4 * ys * lows
    factor = 1.0 / math.sqrt(activations.shape[0] * 2 * near * highs)

    mine = pick(grad_query, grad_key)
    other = pick(grad_key, grad_query)
    activations2, cotangent2 = swap(activations, "c"), swap(other, "c")
    sent = terms(activations2, cotangent2, terms(activations, mine)).astype(jnp.float16)
    landed = exchange(sent.reshape((near,) + sent.shape[4:]), NEAR).astype(jnp.float32)
    summed = (landed[:, :-1] * jnp.exp2(-landed[:, -1:])).sum(axis=0)

    own = pick(w_query, w_key)
    own = lax.dynamic_slice_in_dim(own, lax.axis_index("xh") * half, half, 0)
    high = lax.reduce_precision(summed, 8, 7)
    parts = [copies(own, highs), high.astype(jnp.bfloat16), (summed - high).astype(jnp.bfloat16)]
    landed = exchange(jnp.concatenate(parts, axis=1), "zh")
    column = landed[:, :half]
    summed = landed[:, half:].astype(jnp.float32)
    summed = (summed[:, :half] + summed[:, half:]).sum(axis=0) * factor

    sheet = exchange(copies(column, near), NEAR)
    both = jnp.stack(ordered(summed, swap(summed, "c"), "c"))
    whole = jnp.concatenate(ordered(both, swap(both, "xh"), "xh"), axis=1)
    sheet, whole = lax.optimization_barrier((sheet, whole))
    sheet = sheet.reshape(2, ys, 2, lows, highs, half, head).transpose(1, 4, 3, 2, 0, 5, 6)
    sheet = sheet.reshape(width, head)
    other_sheet = swap(sheet, "c")

    weights = jnp.concatenate([sheet, other_sheet], axis=1)
    cotangent = jnp.concatenate([mine, other], axis=1)
    projected = jnp.dot(activations, weights, preferred_element_type=jnp.float32).astype(jnp.bfloat16)
    grad_input = lax.dot_general(
        cotangent, weights, (((1,), (1,)), ((), ())), preferred_element_type=jnp.float32
    ).astype(jnp.bfloat16)
    first, second = projected[:, :head], projected[:, head:]
    return (pick(first, second), pick(second, first), grad_input, whole[0], whole[1])


def solution(mesh):
    names = ("xh", "c", "y", "zh", "zl", "xl")
    shape = (2, 2, 4, mesh.shape["shard"] // 16, 2, 2)
    fine = Mesh(mesh.devices.reshape(shape), names)
    tokens = P(names, None)
    weights = P(("y", "zh", "zl", "xl"), None)
    return jax.shard_map(
        body,
        mesh=fine,
        in_specs=(tokens, weights, weights, tokens, tokens),
        out_specs=(tokens, tokens, tokens, weights, weights),
        check_vma=False,
    )
```

```python
import math

import jax
import jax.numpy as jnp
from jax import lax
from jax.experimental import pallas as pl
from jax.experimental.pallas import tpu as pltpu
from jax.sharding import Mesh, PartitionSpec as P

NEAR = ("xh", "y", "xl", "zl")


def swap(block, axis):
    return lax.ppermute(block, axis, [(0, 1), (1, 0)])


def ordered(own, came, axis):
    first = lax.axis_index(axis) == 0
    return lax.select(first, own, came), lax.select(first, came, own)


def pick(first, second):
    return lax.select(lax.axis_index("c") == 0, first, second)


def exchange(blocks, axes):
    return lax.all_to_all(blocks, axes, 0, 0, tiled=True)


def copies(block, count):
    return jnp.broadcast_to(block[None], (count,) + block.shape)


def terms_kernel(highs, width, act_ref, cot_ref, *refs):
    out_ref = refs[-1]
    _, ys, _, lows, _, half, head = out_ref.shape
    cut = 2
    span = highs // cut
    block = width // (ys * cut)
    peak = jnp.zeros((half, head), jnp.float32)
    for y in range(ys):
        for z in range(cut):
            start = (y * cut + z) * block
            part = lax.dot_general(
                act_ref[:, start : start + block],
                cot_ref[:, cot_ref.shape[1] - head :],
                (((0,), (0,)), ((), ())),
                preferred_element_type=jnp.float32,
            ).reshape(span, lows, 2, 2, half, head)
            for i in range(2):
                for j in range(2):
                    for low in range(lows):
                        piece = part[:, low, j, i]
                        if len(refs) == 2:
                            piece = piece + refs[0][i, y, j, low, z * span : (z + 1) * span]
                            peak = jnp.maximum(peak, jnp.abs(piece).max(axis=0))
                        out_ref[i, y, j, low, z * span : (z + 1) * span] = piece
    if len(refs) == 2:
        top = jnp.broadcast_to(jnp.max(peak, keepdims=True), (half, head))
        level = jnp.floor(jnp.log2(32768.0 / jnp.maximum(top, 1e-30)))
        scale = jnp.exp2(level)
        for i in range(2):
            for y in range(ys):
                for j in range(2):
                    for low in range(lows):
                        out_ref[i, y, j, low, :highs] = out_ref[i, y, j, low, :highs] * scale[None]
                        out_ref[i, y, j, low, highs] = level


def terms(joined, cotangent, width, head, *others):
    tokens = joined.shape[0]
    ys, lows, highs = (lax.axis_size(a) for a in ("y", "zl", "zh"))
    half = width // (4 * ys * lows * highs)
    return pl.pallas_call(
        lambda *refs: terms_kernel(highs, width, *refs),
        out_shape=jax.ShapeDtypeStruct(
            (2, ys, 2, lows, highs + len(others), half, head), jnp.float32
        ),
        compiler_params=pltpu.CompilerParams(vmem_limit_bytes=40 * 2**20),
        cost_estimate=pl.CostEstimate(
            flops=2 * tokens * width * head, bytes_accessed=6 * width * head, transcendentals=0
        ),
    )(joined, cotangent, *others)


def finish_kernel(core_ref, act_ref, own_ref, came_ref, mine_ref, other_ref, *refs):
    query_ref, key_ref, grad_ref, held_ref, sems = refs
    count = sems.shape[0]
    block = own_ref.shape[0] // count
    sends = []
    for i in range(count):
        span = pl.ds(i * block, block)
        grad = sum(
            lax.dot_general(
                cot[...], weights[span], (((1,), (1,)), ((), ())), preferred_element_type=jnp.float32
            )
            for cot, weights in ((mine_ref, own_ref), (other_ref, came_ref))
        )
        held_ref[:, span] = grad.astype(held_ref.dtype)
        send = pltpu.make_async_copy(held_ref.at[:, span], grad_ref.at[:, span], sems.at[i])
        send.start()
        sends.append(send)
    own, came = (
        jnp.dot(act_ref[...], weights[...], preferred_element_type=jnp.float32).astype(query_ref.dtype)
        for weights in (own_ref, came_ref)
    )

    @pl.when(core_ref[0] == 0)
    def _():
        query_ref[...] = own
        key_ref[...] = came

    @pl.when(core_ref[0] != 0)
    def _():
        query_ref[...] = came
        key_ref[...] = own

    for send in sends:
        send.wait()


def finish(activations, sheet, other_sheet, mine, other):
    tokens, width = activations.shape
    head = sheet.shape[1]
    dtype = activations.dtype
    count = 8
    core = lax.axis_index("c").astype(jnp.int32).reshape(1)
    out = jax.ShapeDtypeStruct((tokens, head), dtype)
    return pl.pallas_call(
        finish_kernel,
        in_specs=[pl.BlockSpec(memory_space=pltpu.SMEM)]
        + [pl.BlockSpec(memory_space=pltpu.VMEM)] * 5,
        out_specs=[pl.BlockSpec(memory_space=pltpu.VMEM)] * 2 + [pl.BlockSpec(memory_space=pl.ANY)],
        out_shape=(out, out, jax.ShapeDtypeStruct((tokens, width), dtype)),
        scratch_shapes=[pltpu.VMEM((tokens, width), dtype), pltpu.SemaphoreType.DMA((count,))],
        compiler_params=pltpu.CompilerParams(vmem_limit_bytes=40 * 2**20),
        cost_estimate=pl.CostEstimate(
            flops=8 * tokens * width * head, bytes_accessed=8 * tokens * width, transcendentals=0
        ),
    )(core, activations, sheet, other_sheet, mine, other)


def body(activations, w_query, w_key, grad_query, grad_key):
    width = activations.shape[1]
    rows, head = w_query.shape
    ys, highs, lows = (lax.axis_size(a) for a in ("y", "zh", "zl"))
    half = rows // 2
    near = 4 * ys * lows
    factor = 1.0 / math.sqrt(activations.shape[0] * 2 * near * highs)

    mine = pick(grad_query, grad_key)
    other = pick(grad_key, grad_query)
    joined = jnp.concatenate([activations, other], axis=1)
    came = swap(joined, "c")
    sent = terms(came, came, width, head, terms(joined, mine, width, head)).astype(jnp.float16)
    landed = exchange(sent.reshape((near,) + sent.shape[4:]), NEAR).astype(jnp.float32)
    summed = (landed[:, :-1] * jnp.exp2(-landed[:, -1:])).sum(axis=0)

    own = pick(w_query, w_key)
    own = lax.dynamic_slice_in_dim(own, lax.axis_index("xh") * half, half, 0)
    high = lax.reduce_precision(summed, 8, 7)
    parts = [copies(own, highs), high.astype(jnp.bfloat16), (summed - high).astype(jnp.bfloat16)]
    landed = exchange(jnp.concatenate(parts, axis=1), "zh")
    column = landed[:, :half]
    summed = landed[:, half:].astype(jnp.float32)
    summed = (summed[:, :half] + summed[:, half:]).sum(axis=0) * factor

    sheet = exchange(copies(column, near), NEAR)
    both = jnp.stack(ordered(summed, swap(summed, "c"), "c"))
    whole = jnp.concatenate(ordered(both, swap(both, "xh"), "xh"), axis=1)
    sheet, whole = lax.optimization_barrier((sheet, whole))
    sheet = sheet.reshape(2, ys, 2, lows, highs, half, head).transpose(1, 4, 3, 2, 0, 5, 6)
    sheet = sheet.reshape(width, head)
    other_sheet = swap(sheet, "c")

    query_out, key_out, grad_input = finish(activations, sheet, other_sheet, mine, other)
    return (query_out, key_out, grad_input, whole[0], whole[1])


def solution(mesh):
    names = ("xh", "c", "y", "zh", "zl", "xl")
    shape = (2, 2, 4, mesh.shape["shard"] // 16, 2, 2)
    fine = Mesh(mesh.devices.reshape(shape), names)
    tokens = P(names, None)
    weights = P(("y", "zh", "zl", "xl"), None)
    return jax.shard_map(
        body,
        mesh=fine,
        in_specs=(tokens, weights, weights, tokens, tokens),
        out_specs=(tokens, tokens, tokens, weights, weights),
        check_vma=False,
    )
```

```python
import math

import jax
import jax.numpy as jnp
from jax import lax
from jax.experimental import pallas as pl
from jax.experimental.pallas import tpu as pltpu
from jax.sharding import Mesh, PartitionSpec as P

NEAR = ("xh", "y", "xl", "zl")


def swap(block, axis):
    return lax.ppermute(block, axis, [(0, 1), (1, 0)])


def ordered(own, came, axis):
    first = lax.axis_index(axis) == 0
    return lax.select(first, own, came), lax.select(first, came, own)


def pick(first, second):
    return lax.select(lax.axis_index("c") == 0, first, second)


def exchange(blocks, axes):
    return lax.all_to_all(blocks, axes, 0, 0, tiled=True)


def copies(block, count):
    return jnp.broadcast_to(block[None], (count,) + block.shape)


def columns(core, width, head):
    return pl.ds(pl.multiple_of(width + core * head, head), head)


def terms_kernel(highs, width, core_ref, act_ref, *refs):
    out_ref = refs[-1]
    _, ys, _, lows, _, half, head = out_ref.shape
    cut = 2
    span = highs // cut
    block = width // (ys * cut)
    cotangent = act_ref[:, columns(core_ref[0], width, head)]
    peak = jnp.zeros((half, head), jnp.float32)
    for y in range(ys):
        for z in range(cut):
            start = (y * cut + z) * block
            part = lax.dot_general(
                act_ref[:, start : start + block],
                cotangent,
                (((0,), (0,)), ((), ())),
                preferred_element_type=jnp.float32,
            ).reshape(span, lows, 2, 2, half, head)
            for i in range(2):
                for j in range(2):
                    for low in range(lows):
                        piece = part[:, low, j, i]
                        if len(refs) == 2:
                            piece = piece + refs[0][i, y, j, low, z * span : (z + 1) * span]
                            peak = jnp.maximum(peak, jnp.abs(piece).max(axis=0))
                        out_ref[i, y, j, low, z * span : (z + 1) * span] = piece
    if len(refs) == 2:
        top = jnp.broadcast_to(jnp.max(peak, keepdims=True), (half, head))
        level = jnp.floor(jnp.log2(32768.0 / jnp.maximum(top, 1e-30)))
        scale = jnp.exp2(level)
        for i in range(2):
            for y in range(ys):
                for j in range(2):
                    for low in range(lows):
                        out_ref[i, y, j, low, :highs] = out_ref[i, y, j, low, :highs] * scale[None]
                        out_ref[i, y, j, low, highs] = level


def terms(core, joined, width, head, *others):
    tokens = joined.shape[0]
    ys, lows, highs = (lax.axis_size(a) for a in ("y", "zl", "zh"))
    half = width // (4 * ys * lows * highs)
    return pl.pallas_call(
        lambda *refs: terms_kernel(highs, width, *refs),
        in_specs=[pl.BlockSpec(memory_space=pltpu.SMEM)]
        + [pl.BlockSpec(memory_space=pltpu.VMEM)] * (1 + len(others)),
        out_shape=jax.ShapeDtypeStruct(
            (2, ys, 2, lows, highs + len(others), half, head), jnp.float32
        ),
        compiler_params=pltpu.CompilerParams(vmem_limit_bytes=40 * 2**20),
        cost_estimate=pl.CostEstimate(
            flops=2 * tokens * width * head, bytes_accessed=6 * width * head, transcendentals=0
        ),
    )(core, joined, *others)


def finish_kernel(core_ref, joined_ref, own_ref, came_ref, *refs):
    query_ref, key_ref, grad_ref, held_ref, sems = refs
    count = sems.shape[0]
    width, head = own_ref.shape
    block = width // count
    core = core_ref[0]
    cotangent = jnp.concatenate(
        [joined_ref[:, columns(index, width, head)] for index in (core, 1 - core)], axis=1
    )
    projected = jnp.zeros((joined_ref.shape[0], 2 * head), jnp.float32)
    sends = []
    for i in range(count):
        span = pl.ds(i * block, block)
        weights = jnp.concatenate([own_ref[span], came_ref[span]], axis=1)
        grad = lax.dot_general(
            cotangent, weights, (((1,), (1,)), ((), ())), preferred_element_type=jnp.float32
        )
        held_ref[:, span] = grad.astype(held_ref.dtype)
        send = pltpu.make_async_copy(held_ref.at[:, span], grad_ref.at[:, span], sems.at[i])
        send.start()
        sends.append(send)
        projected += jnp.dot(joined_ref[:, span], weights, preferred_element_type=jnp.float32)
    projected = projected.astype(query_ref.dtype)
    own, came = projected[:, :head], projected[:, head:]

    @pl.when(core_ref[0] == 0)
    def _():
        query_ref[...] = own
        key_ref[...] = came

    @pl.when(core_ref[0] != 0)
    def _():
        query_ref[...] = came
        key_ref[...] = own

    for send in sends:
        send.wait()


def finish(core, joined, sheet, other_sheet):
    tokens = joined.shape[0]
    width, head = sheet.shape
    dtype = joined.dtype
    count = 8
    out = jax.ShapeDtypeStruct((tokens, head), dtype)
    return pl.pallas_call(
        finish_kernel,
        in_specs=[pl.BlockSpec(memory_space=pltpu.SMEM)]
        + [pl.BlockSpec(memory_space=pltpu.VMEM)] * 3,
        out_specs=[pl.BlockSpec(memory_space=pltpu.VMEM)] * 2 + [pl.BlockSpec(memory_space=pl.ANY)],
        out_shape=(out, out, jax.ShapeDtypeStruct((tokens, width), dtype)),
        scratch_shapes=[pltpu.VMEM((tokens, width), dtype), pltpu.SemaphoreType.DMA((count,))],
        compiler_params=pltpu.CompilerParams(vmem_limit_bytes=40 * 2**20),
        cost_estimate=pl.CostEstimate(
            flops=8 * tokens * width * head, bytes_accessed=8 * tokens * width, transcendentals=0
        ),
    )(core, joined, sheet, other_sheet)


def body(activations, w_query, w_key, grad_query, grad_key):
    width = activations.shape[1]
    rows, head = w_query.shape
    ys, highs, lows = (lax.axis_size(a) for a in ("y", "zh", "zl"))
    half = rows // 2
    near = 4 * ys * lows
    factor = 1.0 / math.sqrt(activations.shape[0] * 2 * near * highs)

    core = lax.axis_index("c").astype(jnp.int32).reshape(1)
    joined = jnp.concatenate([activations, grad_query, grad_key], axis=1)
    came = swap(joined, "c")
    sent = terms(core, came, width, head, terms(core, joined, width, head)).astype(jnp.float16)
    landed = exchange(sent.reshape((near,) + sent.shape[4:]), NEAR).astype(jnp.float32)
    summed = (landed[:, :-1] * jnp.exp2(-landed[:, -1:])).sum(axis=0)

    own = pick(w_query, w_key)
    own = lax.dynamic_slice_in_dim(own, lax.axis_index("xh") * half, half, 0)
    high = lax.reduce_precision(summed, 8, 7)
    parts = [copies(own, highs), high.astype(jnp.bfloat16), (summed - high).astype(jnp.bfloat16)]
    landed = exchange(jnp.concatenate(parts, axis=1), "zh")
    column = landed[:, :half]
    summed = landed[:, half:].astype(jnp.float32)
    summed = (summed[:, :half] + summed[:, half:]).sum(axis=0) * factor

    sheet = exchange(copies(column, near), NEAR)
    both = jnp.stack(ordered(summed, swap(summed, "c"), "c"))
    whole = jnp.concatenate(ordered(both, swap(both, "xh"), "xh"), axis=1)
    sheet, whole = lax.optimization_barrier((sheet, whole))
    sheet = sheet.reshape(2, ys, 2, lows, highs, half, head).transpose(1, 4, 3, 2, 0, 5, 6)
    sheet = sheet.reshape(width, head)
    other_sheet = swap(sheet, "c")

    query_out, key_out, grad_input = finish(core, joined, sheet, other_sheet)
    return (query_out, key_out, grad_input, whole[0], whole[1])


def solution(mesh):
    names = ("xh", "c", "y", "zh", "zl", "xl")
    shape = (2, 2, 4, mesh.shape["shard"] // 16, 2, 2)
    fine = Mesh(mesh.devices.reshape(shape), names)
    tokens = P(names, None)
    weights = P(("y", "zh", "zl", "xl"), None)
    return jax.shard_map(
        body,
        mesh=fine,
        in_specs=(tokens, weights, weights, tokens, tokens),
        out_specs=(tokens, tokens, tokens, weights, weights),
        check_vma=False,
    )
```
